128 devices in a mesh: section: 4 (over z_hi, core), ctx: 32 (over z_lo, x, y).
Axes of the slice: x: 4, y: 4, z: 4 (z_hi: 2, z_lo: 2; z = z_hi * 2 + z_lo), core: 2. Of those that a mesh axis runs over, the one named last changes fastest.
Arguments:
- queries: bfloat16 [4, 16384, 1024], P('section', 'ctx'), may hold values from -6 to 6
- keys: bfloat16 [4, 16384, 128], P('section', 'ctx'), may hold values from -6 to 6
- values: bfloat16 [4, 16384, 128], P('section', 'ctx'), may hold values from -6 to 6
- outputs: bfloat16 [4, 16384, 1024], P('section', 'ctx'), may hold values from -6 to 6
- out_grads: bfloat16 [4, 16384, 1024], P('section', 'ctx'), may hold values from -12 to 12
- lse: float32 [4, 16384, 8], P('section', 'ctx')
- doc_start: int32 [4, 16384], P('section', 'ctx'), may hold values from 0 to 16383, as said below
Outputs:
- query_grads: bfloat16 [4, 16384, 1024], P('section', 'ctx')
- key_grads: bfloat16 [4, 16384, 128], P('section', 'ctx')
- value_grads: bfloat16 [4, 16384, 128], P('section', 'ctx')
The draws below stay inside these ranges and needn't reach their ends.
Inputs may be any that keep to these rules, and one draw needn't show every extreme that they name: Per section, documents are contiguous: doc_start never falls, doc_start[i] <= i, and each document has 1 to 3584 tokens; the first document has exactly 3584.
All inputs are finite; a program needn't handle non-finite values.
Results may differ from the reference program's by a relative error of at most 0.0055.
Values may be sent and summed in bfloat16 or wider, within the bound.
No kernel may reach another device: no remote copies, remote signals or barrier semaphores. Data moves between devices by JAX's collectives and lax.ppermute only.
A program may use at most 128 MiB of HBM per device.

```python
import jax
import jax.numpy as jnp
from jax import lax

HEADS = 8
HD = 128
TOK_DEV = 512
STEPS = 8
SECTIONS = 4
TOKENS = 16384
MOST = 3584


def starts_single(key):
    lengths = jax.random.randint(key, (TOKENS,), 1, MOST + 1)
    lengths = lengths.at[0].set(MOST)
    ends = jnp.cumsum(lengths)
    places = jnp.arange(TOKENS, dtype=jnp.int32)
    which = jnp.searchsorted(ends, places, side='right')
    begins = (ends - lengths).astype(jnp.int32)
    return begins[which]


def doc_layout(key):
    section_keys = jax.random.split(key, SECTIONS)
    return jax.vmap(starts_single)(section_keys)


def draw_doc_start(key, part):
    return doc_layout(key).astype(jnp.int32)


def draw_lse(key, part):
    begins = doc_layout(key)
    key = jax.random.fold_in(key, 7)
    within = (jnp.arange(TOKENS, dtype=jnp.int32)[None, :] - begins).astype(jnp.float32)
    noise = jax.random.uniform(key, (SECTIONS, TOKENS, HEADS), jnp.float32, 0.5, 1.5)
    return (jnp.log1p(within)[:, :, None] + noise).astype(jnp.float32)


def levels(key, dims, cuts, smallest, top_value):
    factor_of = 1.0
    for position, shards_of in cuts:
        heights = jax.random.uniform(jax.random.fold_in(jax.random.fold_in(key, 6), position), (shards_of,), jnp.float32, smallest / len(cuts), top_value / len(cuts))
        factor_of = factor_of * jnp.repeat(jnp.exp(heights), dims[position] // shards_of).reshape((-1,) + (1,) * (len(dims) - 1 - position))
    return factor_of


def centred(key, shape, width, limit, cuts=(), held_as=jnp.bfloat16):
    array = jax.random.normal(key, shape, jnp.float32) * width
    if len(cuts) > 0:
        array = levels(key, shape, cuts, -0.22, 0.18) * array
    return jnp.clip(array, min=-limit, max=limit).astype(held_as)


def setup_inputs(seed: int = 0) -> dict:
    key_of = jax.random.split(jax.random.key(seed), 8)
    return {
        "queries": centred(key_of[0], (SECTIONS, TOKENS, HEADS * HD), 1.0, 6.0, ((0, 4), (1, 32))),
        "keys": centred(key_of[1], (SECTIONS, TOKENS, HD), 1.0, 6.0, ((0, 4), (1, 32))),
        "values": centred(key_of[2], (SECTIONS, TOKENS, HD), 1.0, 6.0, ((0, 4), (1, 32))),
        "outputs": centred(key_of[3], (SECTIONS, TOKENS, HEADS * HD), 1.0, 6.0, ((0, 4), (1, 32))),
        "out_grads": centred(key_of[4], (SECTIONS, TOKENS, HEADS * HD), 2.0, 12.0, ((0, 4), (1, 32))),
        "lse": draw_lse(jax.random.fold_in(key_of[7], 71), 0),
        "doc_start": draw_doc_start(jax.random.fold_in(key_of[7], 71), 0),
    }


def block_terms(query_blk, dout_blk, lse_rows, delta, key_blk, value_blk, visible):
    scale = query_blk.shape[-1] ** -0.5
    query_f = query_blk.astype(jnp.float32)
    dout_f = dout_blk.astype(jnp.float32)
    key_f = key_blk.astype(jnp.float32)
    value_f = value_blk.astype(jnp.float32)
    scores = jnp.einsum('qhd,kd->hqk', query_f, key_f)
    prob = jnp.where(visible[None], jnp.exp(scores * scale - lse_rows.T[:, :, None]), jnp.float32(0.0))
    prob_b = prob.astype(jnp.bfloat16).astype(jnp.float32)
    value_g = jnp.einsum('hqk,qhd->kd', prob_b, dout_f)
    dprob = jnp.einsum('qhd,kd->hqk', dout_f, value_f)
    dscore = (prob * (dprob - delta.T[:, :, None]) * scale).astype(jnp.bfloat16).astype(jnp.float32)
    query_g = jnp.einsum('hqk,kd->qhd', dscore, key_f)
    key_g = jnp.einsum('hqk,qhd->kd', dscore, query_f)
    return query_g, key_g, value_g


def one_section(queries, keys, values, outputs, out_grads, lse, doc_start):
    total = queries.shape[0]
    heads = lse.shape[1]
    head_size = keys.shape[1]
    blocks = total // TOK_DEV
    query_all = queries.reshape(total, heads, head_size)
    dout_all = out_grads.reshape(total, heads, head_size)
    delta_all = jnp.sum(dout_all.astype(jnp.float32) * outputs.reshape(total, heads, head_size).astype(jnp.float32), axis=-1)
    margin = (STEPS - 1) * TOK_DEV
    key_pad = jnp.concatenate([jnp.zeros((margin, head_size), keys.dtype), keys], axis=0)
    value_pad = jnp.concatenate([jnp.zeros((margin, head_size), values.dtype), values], axis=0)
    places = jnp.arange(TOK_DEV, dtype=jnp.int32)

    def per_block(carry, block):
        key_acc, value_acc = carry
        first = (block * TOK_DEV).astype(jnp.int32)
        query_blk = lax.dynamic_slice_in_dim(query_all, first, TOK_DEV, 0)
        dout_blk = lax.dynamic_slice_in_dim(dout_all, first, TOK_DEV, 0)
        lse_rows = lax.dynamic_slice_in_dim(lse, first, TOK_DEV, 0)
        delta = lax.dynamic_slice_in_dim(delta_all, first, TOK_DEV, 0)
        start_q = lax.dynamic_slice_in_dim(doc_start, first, TOK_DEV, 0)
        pos_q = first + places
        query_sum = jnp.zeros((TOK_DEV, heads, head_size), jnp.float32)
        for step in range(STEPS):
            owner = (block - step).astype(jnp.int32)
            offset = ((owner + STEPS - 1) * TOK_DEV).astype(jnp.int32)
            key_blk = lax.dynamic_slice_in_dim(key_pad, offset, TOK_DEV, 0)
            value_blk = lax.dynamic_slice_in_dim(value_pad, offset, TOK_DEV, 0)
            pos_k = owner * TOK_DEV + places
            visible = (pos_k[None, :] >= start_q[:, None]) & (pos_k[None, :] <= pos_q[:, None])
            active = (owner >= 0) & (owner * TOK_DEV + TOK_DEV - 1 >= start_q[0])

            def compute(unused):
                return block_terms(query_blk, dout_blk, lse_rows, delta, key_blk, value_blk, visible)

            def nothing(unused):
                return (jnp.zeros((TOK_DEV, heads, head_size), jnp.float32), jnp.zeros((TOK_DEV, head_size), jnp.float32), jnp.zeros((TOK_DEV, head_size), jnp.float32))

            terms = lax.cond(active, compute, nothing, 0)
            query_sum = query_sum + terms[0]
            key_acc = lax.dynamic_update_slice_in_dim(key_acc, lax.dynamic_slice_in_dim(key_acc, offset, TOK_DEV, 0) + terms[1], offset, 0)
            value_acc = lax.dynamic_update_slice_in_dim(value_acc, lax.dynamic_slice_in_dim(value_acc, offset, TOK_DEV, 0) + terms[2], offset, 0)
        return (key_acc, value_acc), query_sum

    start_acc = (jnp.zeros((total + margin, head_size), jnp.float32), jnp.zeros((total + margin, head_size), jnp.float32))
    (key_acc, value_acc), query_parts = lax.scan(per_block, start_acc, jnp.arange(blocks, dtype=jnp.int32))
    query_grads = query_parts.reshape(total, heads * head_size).astype(jnp.bfloat16)
    return query_grads, key_acc[margin:].astype(jnp.bfloat16), value_acc[margin:].astype(jnp.bfloat16)


def reference(queries, keys, values, outputs, out_grads, lse, doc_start):
    def run(pieces):
        return one_section(*pieces)

    query_grads, key_grads, value_grads = lax.map(run, (queries, keys, values, outputs, out_grads, lse, doc_start))
    return (jnp.roll(query_grads, -1, axis=0), jnp.roll(key_grads, -1, axis=0), jnp.roll(value_grads, -1, axis=0))
```

```python
import math

import jax
import jax.numpy as jnp
from jax import lax
from jax.experimental import pallas as pl
from jax.experimental.pallas import tpu as pltpu
from jax.sharding import PartitionSpec as P

HEADS = 8
HD = 128
ROWS = 512
HALF = 256
STEPS = 8
SCALE = HD**-0.5
LOG2E = math.log2(math.e)
GROUPS = ((7, 6), (5, 4), (3, 2))
HEAD_GROUPS = ((0, 4), (4, 8))
LAST = 1
F32 = jnp.float32
BF16 = jnp.bfloat16
SMEM = pltpu.SMEM
VMEM = pltpu.VMEM


def dot(a, b, da, db):
    return lax.dot_general(a, b, (((da,), (db,)), ((), ())), preferred_element_type=F32)


def tile(refs, heads, keys_at, n_keys, rows, bias):
    q_ref, do_ref, ld_ref, kv_ref, kt_ref, dq_ref, dk_ref, dv_ref = refs
    here = pl.ds(keys_at, n_keys)
    k = kv_ref[here, :HD]
    v = kv_ref[here, HD:]
    kt = kt_ref[:, here]
    for n, h in enumerate(heads):
        cols = slice(n * HD, (n + 1) * HD)
        q = q_ref[rows, cols]
        do = do_ref[rows, cols]
        x = dot(k, q, 1, 1) * (SCALE * LOG2E) - ld_ref[h : h + 1, rows]
        if bias is not None:
            x = x + bias[...]
        p = jnp.exp2(x)
        dp = dot(v, do, 1, 1)
        ds = (p * (dp - ld_ref[HEADS + h : HEADS + h + 1, rows])).astype(BF16)
        dv_ref[here, :] += dot(p.astype(BF16), do, 1, 0)
        dk_ref[here, :] += dot(ds, q, 1, 0)
        dq_ref[cols, rows] += dot(kt, ds, 1, 0)


def block(d, heads, base, starts, start_row, refs, bias_ref):
    kv_ref, kt_ref, dk_ref, dv_ref = refs[3], refs[4], refs[6], refs[7]
    first_key = base - d * ROWS
    there = first_key >= 0
    dk_ref[...] = jnp.zeros_like(dk_ref)
    dv_ref[...] = jnp.zeros_like(dv_ref)
    active = there & (first_key + ROWS - 1 >= starts[0, 0])
    whole = first_key >= starts[0, ROWS - 1] if d else False

    def masked(keys_at, q_at):
        rows = slice(q_at, ROWS) if not isinstance(q_at, slice) else q_at
        n = rows.stop - rows.start
        at = first_key + keys_at
        key = lax.broadcasted_iota(jnp.int32, (HALF, n), 0) + at
        ok = key >= start_row[:, rows]
        if d == 0:
            own = lax.broadcasted_iota(jnp.int32, (HALF, n), 1) + (base + rows.start)
            ok = ok & (key <= own)
        bias = bias_ref.at[:, :n]
        bias[...] = jnp.where(ok, 0.0, -1e30)
        tile(refs, heads, keys_at, HALF, rows, bias)

    @pl.when(active)
    def _():
        kt_ref[...] = kv_ref[:, :HD].T

        if d == 0:
            masked(0, slice(0, ROWS))
            masked(HALF, slice(HALF, ROWS))
        else:

            @pl.when(whole)
            def _():
                tile(refs, heads, 0, ROWS, slice(0, ROWS), None)

            @pl.when(jnp.logical_not(whole))
            def _():
                def part(i, carry):
                    keys_at = pl.multiple_of(i * HALF, HALF)
                    top = first_key + keys_at + HALF - 1
                    both = top >= starts[0, HALF]

                    @pl.when(both)
                    def _():
                        masked(keys_at, slice(0, ROWS))

                    @pl.when(jnp.logical_not(both) & (top >= starts[0, 0]))
                    def _():
                        masked(keys_at, slice(0, HALF))

                    return carry

                lax.fori_loop(0, ROWS // HALF, part, 0)


def give(out_ref, dk_ref, dv_ref):
    out_ref[:, :HD] = (dk_ref[...] * SCALE).astype(out_ref.dtype)
    out_ref[:, HD:] = dv_ref[...].astype(out_ref.dtype)


def first_kernel(base_ref, starts, start_row, q_ref, do_ref, o_ref, lse_ref, kv_ref, dq_ref, ld_ref, out_ref, kt_ref, dk_ref, dv_ref, bias_ref):
    base = base_ref[0]
    ld_ref[:HEADS, :] = lse_ref[...] * LOG2E
    ones = jnp.ones((8, HD), BF16)
    for h in range(HEADS):
        cols = slice(h * HD, (h + 1) * HD)
        x = do_ref[:, cols].astype(F32) * o_ref[:, cols].astype(F32)
        hi = x.astype(BF16)
        lo = (x - hi.astype(F32)).astype(BF16)
        row = dot(ones, hi, 1, 1) + dot(ones, lo, 1, 1)
        ld_ref[HEADS + h : HEADS + h + 1, :] = row[:1]
    dq_ref[...] = jnp.zeros_like(dq_ref)
    refs = (q_ref, do_ref, ld_ref, kv_ref, kt_ref, dq_ref, dk_ref, dv_ref)
    block(0, range(HEADS), base, starts, start_row, refs, bias_ref)
    give(out_ref, dk_ref, dv_ref)


def middle_kernel(ds, base_ref, starts, start_row, q_ref, do_ref, ld_ref, *rest):
    n = len(ds)
    kv_refs, rest = rest[:n], rest[n + 1 :]
    dq_ref, out_refs, rest = rest[0], rest[1 : n + 1], rest[n + 1 :]
    kt_ref, dk_ref, dv_ref, bias_ref = rest
    for d, kv_ref, out_ref in zip(ds, kv_refs, out_refs):
        refs = (q_ref, do_ref, ld_ref, kv_ref, kt_ref, dq_ref, dk_ref, dv_ref)
        block(d, range(HEADS), base_ref[0], starts, start_row, refs, bias_ref)
        give(out_ref, dk_ref, dv_ref)


def last_kernel(first, last, d, base_ref, starts, start_row, q_ref, do_ref, ld_ref, kv_ref, dq_in, q_out, kv_out, kt_ref, dk_ref, dv_ref, bias_ref, dq_ref):
    n = last - first
    dq_ref[...] = dq_in[...]
    refs = (q_ref, do_ref, ld_ref, kv_ref, kt_ref, dq_ref, dk_ref, dv_ref)
    block(d, range(first, last), base_ref[0], starts, start_row, refs, bias_ref)
    kv_out[:, :HD] = dk_ref[...] * SCALE
    kv_out[:, HD:] = dv_ref[...]
    for h in range(n):
        cols = slice(h * HD, (h + 1) * HD)
        q_out[:, cols] = (dq_ref[cols, :] * SCALE).astype(BF16).T


def work(pairs):
    flops = int(pairs * 5 * 2 * ROWS * ROWS * HD * HEADS)
    return pl.CostEstimate(flops=flops, bytes_accessed=1 << 20, transcendentals=0)


def vmem(shape, dtype):
    return pltpu.VMEM(shape, dtype)


SCRATCH = [
    vmem((HD, ROWS), BF16),
    vmem((ROWS, HD), F32),
    vmem((ROWS, HD), F32),
    vmem((HALF, ROWS), F32),
]


def in_smem(n):
    return [pl.BlockSpec(memory_space=SMEM)] * n


def in_vmem(n):
    return [pl.BlockSpec(memory_space=VMEM)] * n


def shape(dims, dtype):
    return jax.ShapeDtypeStruct(dims, dtype)


PARAMS = pltpu.CompilerParams(vmem_limit_bytes=24 << 20)


def shifted(block, axis, distance):
    devices = range(lax.axis_size(axis))
    route = [((i - distance) % len(devices), i) for i in devices]
    return lax.ppermute(block, axis, route)


def per_device(queries, keys, values, outputs, out_grads, lse, doc_start):
    q, do, o = queries[0], out_grads[0], outputs[0]
    base = (lax.axis_index("ctx") * ROWS).astype(jnp.int32)[None]
    common = (base, doc_start, doc_start)
    kv = jnp.concatenate([keys[0], values[0]], axis=1)
    order = [d for ds in GROUPS for d in ds] + [LAST]
    held = {d: shifted(kv, "ctx", d) for d in order}
    wide = shape((HEADS * HD, ROWS), F32)
    dq, ld, own = pl.pallas_call(
        first_kernel,
        out_shape=[wide, shape((2 * HEADS, ROWS), F32), shape((ROWS, 2 * HD), F32)],
        in_specs=in_smem(2) + in_vmem(6),
        out_specs=in_vmem(3),
        scratch_shapes=SCRATCH,
        compiler_params=PARAMS,
        cost_estimate=work(0.75),
        name="own_block",
    )(*common, q, do, o, lse[0].T, kv)
    parts = {}
    for ds in GROUPS:
        n = len(ds)
        dq, *outs = pl.pallas_call(
            lambda *refs, ds=ds: middle_kernel(ds, *refs),
            out_shape=[wide] + [shape((ROWS, 2 * HD), BF16)] * n,
            in_specs=in_smem(2) + in_vmem(5 + n),
            out_specs=in_vmem(1 + n),
            input_output_aliases={6 + n: 0},
            scratch_shapes=SCRATCH,
            compiler_params=PARAMS,
            cost_estimate=work(n),
            name="blocks_" + "_".join(map(str, ds)),
        )(*common, q, do, ld, *[held[d] for d in ds], dq)
        for d, out in zip(ds, outs):
            parts[d] = shifted(out, "ctx", -d)
    handed = []
    kv_last = None
    for first, last in HEAD_GROUPS:
        n = last - first
        cols = slice(first * HD, last * HD)
        q_out, kv_out = pl.pallas_call(
            lambda *refs, first=first, last=last: last_kernel(first, last, LAST, *refs),
            out_shape=[shape((ROWS, n * HD), BF16), shape((ROWS, 2 * HD), F32)],
            in_specs=in_smem(2) + in_vmem(6),
            out_specs=in_vmem(2),
            scratch_shapes=SCRATCH + [vmem((n * HD, ROWS), F32)],
            compiler_params=PARAMS,
            cost_estimate=work(n / HEADS),
            name="last_%d" % first,
        )(*common, q[:, cols], do[:, cols], ld, held[LAST], dq[cols])
        handed.append(shifted(q_out, "section", -1))
        kv_last = kv_out if kv_last is None else kv_last + kv_out
    parts[LAST] = shifted(kv_last.astype(BF16), "ctx", -LAST)
    total = own
    for part in parts.values():
        total = total + part.astype(F32)
    kv_g = shifted(total.astype(BF16), "section", -1)
    return (jnp.concatenate(handed, axis=1)[None], kv_g[None, :, :HD], kv_g[None, :, HD:])


def solution(mesh):
    wide = P("section", "ctx", None)
    in_specs = (wide, wide, wide, wide, wide, wide, P("section", "ctx"))
    return jax.shard_map(per_device, mesh=mesh, in_specs=in_specs, out_specs=(wide, wide, wide), check_vma=False)
```

```python
import math

import jax
import jax.numpy as jnp
from jax import lax
from jax.experimental import pallas as pl
from jax.experimental.pallas import tpu as pltpu
from jax.sharding import PartitionSpec as P

HEADS = 8
HD = 128
ROWS = 512
HALF = 256
SCALE = HD**-0.5
LOG2E = math.log2(math.e)
F32 = jnp.float32
BF16 = jnp.bfloat16
LSE, DELTA, LSE_BACK = 0, HEADS, 2 * HEADS
WIDE = jax.ShapeDtypeStruct((HEADS * HD, ROWS), F32)
PAIR = jax.ShapeDtypeStruct((ROWS, 2 * HD), F32)


def dot(a, b, da, db):
    return lax.dot_general(a, b, (((da,), (db,)), ((), ())), preferred_element_type=F32)


def lanes(h):
    return pl.ds(pl.multiple_of(h * HD, HD), HD)


def terms(refs, h, to_h, lse_at, keys_at, n_keys, rows, ok):
    q_ref, do_ref, ld_ref, kv_ref, kt_ref, dq_ref, dk_ref, dv_ref = refs
    here = pl.ds(keys_at, n_keys)
    q = q_ref[rows, lanes(h)]
    do = do_ref[rows, lanes(h)]
    x = dot(kv_ref[here, :HD], q, 1, 1) * (SCALE * LOG2E) - ld_ref[pl.ds(lse_at + h, 1), rows]
    p = jnp.exp2(x)
    if ok is not None:
        p = jnp.where(ok, p, 0.0)
    dp = dot(kv_ref[here, HD:], do, 1, 1) - ld_ref[pl.ds(DELTA + h, 1), rows]
    ds = (p * dp).astype(BF16)
    dv_ref[here, :] += dot(p.astype(BF16), do, 1, 0)
    dk_ref[here, :] += dot(ds, q, 1, 0)
    dq_ref[lanes(to_h), rows] += dot(kt_ref[:, here], ds, 1, 0)


def finish(dq_ref, q_out):
    for h in range(q_out.shape[1] // HD):
        cols = slice(h * HD, (h + 1) * HD)
        q_out[:, cols] = (dq_ref[cols, :] * SCALE).astype(BF16).T


def own_terms(first, n, to, start_row, base, refs):
    kv_ref, kt_ref = refs[3], refs[4]
    kt_ref[...] = kv_ref[:, :HD].T

    def head(h, carry):
        for at, rows in ((0, slice(0, ROWS)), (HALF, slice(HALF, ROWS))):
            n_rows = rows.stop - rows.start
            key = lax.broadcasted_iota(jnp.int32, (HALF, n_rows), 0)
            ok = key >= start_row[:, rows] - (base + at)
            ok = ok & (key + (at - rows.start) <= lax.broadcasted_iota(jnp.int32, (HALF, n_rows), 1))
            terms(refs, h, h - to, LSE, at, HALF, rows, ok)
        return carry

    lax.fori_loop(first, first + n, head, 0)


def first_kernel(n, base_ref, starts, start_row, q_ref, do_ref, o_ref, lse_ref, kv_ref, dq_ref, ld_ref, out_ref, kt_ref, dk_ref, dv_ref):
    lse = lse_ref[...] * LOG2E
    ld_ref[LSE : LSE + HEADS, :] = lse
    ld_ref[LSE_BACK : LSE_BACK + HEADS, :] = jnp.where(start_row[...] == starts[0, 0], lse, 1e30)
    ones = jnp.ones((8, HD), BF16)
    for h in range(HEADS):
        cols = slice(h * HD, (h + 1) * HD)
        x = do_ref[:, cols].astype(F32) * o_ref[:, cols].astype(F32)
        hi = x.astype(BF16)
        lo = (x - hi.astype(F32)).astype(BF16)
        row = dot(ones, hi, 1, 1) + dot(ones, lo, 1, 1)
        ld_ref[DELTA + h : DELTA + h + 1, :] = row[:1]
    dq_ref[...] = jnp.zeros_like(dq_ref)
    dk_ref[...] = jnp.zeros_like(dk_ref)
    dv_ref[...] = jnp.zeros_like(dv_ref)
    own_terms(0, n, 0, start_row, base_ref[0], (q_ref, do_ref, ld_ref, kv_ref, kt_ref, dq_ref, dk_ref, dv_ref))
    out_ref[:, :HD] = dk_ref[...]
    out_ref[:, HD:] = dv_ref[...]


def final_kernel(first, n, base_ref, starts, start_row, q_ref, do_ref, ld_ref, kv_ref, dq_in, sum_in, *rest):
    q_out, out_ref, dq_ref, kt_ref, dk_ref, dv_ref = rest[-6:]
    dq_ref[...] = dq_in[first * HD : (first + n) * HD, :]
    dk_ref[...] = sum_in[:, :HD]
    dv_ref[...] = sum_in[:, HD:]
    own_terms(first, n, first, start_row, base_ref[0], (q_ref, do_ref, ld_ref, kv_ref, kt_ref, dq_ref, dk_ref, dv_ref))
    finish(dq_ref, q_out)
    out_ref[:, :HD] = dk_ref[...] * SCALE
    out_ref[:, HD:] = dv_ref[...]


def back_kernel(ds, first, n, emit, has_sum, sum_out, extra, base_ref, starts, start_row, q_ref, do_ref, ld_ref, dq_in, *rest):
    m = len(ds)
    kv_refs, rest = rest[:m], rest[m:]
    sum_in = rest[0] if has_sum else None
    rest = rest[has_sum + extra :]
    head_out, out_refs, rest = rest[0], rest[1 : m + 1], rest[m + 1 :]
    kv_ref, kt_ref, dk_ref, dv_ref, *rest = rest
    base, start = base_ref[0], starts[0, 0]
    if emit:
        dq_ref, to = rest[0], first
        dq_ref[...] = dq_in[first * HD : (first + n) * HD, :]
    else:
        dq_ref, to = head_out, 0
    if has_sum:
        dk_ref[...] = sum_in[:, :HD]
        dv_ref[...] = sum_in[:, HD:]
    else:
        dk_ref[...] = jnp.zeros_like(dk_ref)
        dv_ref[...] = jnp.zeros_like(dv_ref)
    reach = lax.shift_right_logical(base - start + (ROWS - 1), 9)
    skipped = jnp.clip(ds[0] - reach, 0, m)
    refs = (q_ref, do_ref, ld_ref, kv_ref, kt_ref, dq_ref, dk_ref, dv_ref)

    def seen(d, width):
        key = lax.broadcasted_iota(jnp.int32, (ROWS, width), 0)
        return key >= start - (base - d * ROWS)

    @pl.when(skipped < m)
    def _():
        for b, d in enumerate(ds):
            here = slice(b * ROWS, (b + 1) * ROWS)
            kv = kv_refs[b][...].astype(F32)
            kv_ref[here, :] = jnp.where(seen(d, 2 * HD), kv, kv[ROWS - 1 :, :]).astype(BF16)
            kt_ref[:, here] = jnp.where(seen(d, HD), kv[:, :HD], 0.0).astype(BF16).T

        def step(w, carry):
            w = w * 2
            keys_at = pl.multiple_of((skipped + w // n) * ROWS, ROWS)
            for h in (first + w % n, first + w % n + 1):
                terms(refs, h, h - to, LSE_BACK, keys_at, ROWS, slice(0, ROWS), None)
            return carry

        lax.fori_loop(0, (m - skipped) * (n // 2), step, 0)

    for b, d in enumerate(ds):
        here = slice(b * ROWS, (b + 1) * ROWS)
        if sum_out:
            out_refs[b][:, :HD] = dk_ref[here, :]
            out_refs[b][:, HD:] = dv_ref[here, :]
        else:
            ok = seen(d, HD)
            out_refs[b][:, :HD] = jnp.where(ok, dk_ref[here, :] * SCALE, 0.0).astype(BF16)
            out_refs[b][:, HD:] = jnp.where(ok, dv_ref[here, :], 0.0).astype(BF16)
    if emit:
        finish(dq_ref, head_out)


def work(pairs):
    flops = int(pairs * 5 * 2 * ROWS * ROWS * HD * HEADS)
    return pl.CostEstimate(flops=flops, bytes_accessed=1 << 20, transcendentals=0)


def scratch(m):
    return [pltpu.VMEM((HD, m * ROWS), BF16), pltpu.VMEM((m * ROWS, HD), F32), pltpu.VMEM((m * ROWS, HD), F32)]


def call(kernel, name, pairs, operands, outs, scratch_shapes, extra=(), aliases=None):
    return pl.pallas_call(
        kernel,
        out_shape=outs,
        in_specs=[pl.BlockSpec(memory_space=pltpu.SMEM)] * 2
        + [pl.BlockSpec(memory_space=pltpu.VMEM)] * (len(operands) - 2)
        + [pl.BlockSpec(memory_space=pl.ANY)] * len(extra),
        out_specs=[pl.BlockSpec(memory_space=pltpu.VMEM)] * len(outs),
        input_output_aliases=aliases or {},
        scratch_shapes=scratch_shapes,
        compiler_params=pltpu.CompilerParams(vmem_limit_bytes=24 << 20),
        cost_estimate=work(pairs),
        name=name,
    )(*operands, *extra)


def shifted(block, axis, distance):
    devices = range(lax.axis_size(axis))
    route = [((i - distance) % len(devices), i) for i in devices]
    return lax.ppermute(block, axis, route)


def per_device(queries, keys, values, outputs, out_grads, lse, doc_start):
    q, do, o = queries[0], out_grads[0], outputs[0]
    base = (lax.axis_index("ctx") * ROWS).astype(jnp.int32)[None]
    common = (base, doc_start, doc_start, q, do)
    kv = jnp.concatenate([keys[0], values[0]], axis=1)
    held = {d: shifted(kv, "ctx", d) for d in (6, 7, 5, 4, 3, 2, 1)}
    part = jax.ShapeDtypeStruct((ROWS, 2 * HD), BF16)
    split = HEADS // 2
    half = jax.ShapeDtypeStruct((ROWS, split * HD), BF16)
    stats = jax.ShapeDtypeStruct((3 * HEADS, ROWS), F32)
    own_scratch = scratch(1)

    def first(*refs):
        first_kernel(split, *refs)

    dq, ld, own = call(first, "own_first", 0.4, (*common, o, lse[0].T, kv), [WIDE, stats, PAIR], own_scratch)

    def back(ds, dq, first=0, n=HEADS, emit=False, sum_in=None, sum_out=False, extra=()):
        m = len(ds)
        sums = () if sum_in is None else (sum_in,)

        def kernel(*refs):
            back_kernel(ds, first, n, emit, len(sums), sum_out, len(extra), *refs)

        head = jax.ShapeDtypeStruct((ROWS, n * HD), BF16) if emit else WIDE
        last = [pltpu.VMEM((n * HD, ROWS), F32)] if emit else []
        return call(
            kernel,
            "back_%s_%d" % ("_".join(map(str, ds)), first),
            m * n / HEADS,
            (*common, ld, dq, *[held[d] for d in ds], *sums),
            [head] + [PAIR if sum_out else part] * m,
            [pltpu.VMEM((m * ROWS, 2 * HD), BF16)] + scratch(m) + last,
            extra,
            {} if emit else {6: 0},
        )

    got = {}

    def give_back(ds, outs):
        for d, out in zip(ds, outs):
            got[d] = shifted(out, "ctx", -d)

    dq, *outs = back((7, 6), dq)
    give_back((7, 6), outs)
    dq, *outs = back((5, 4), dq)
    give_back((5, 4), outs)
    dq, *outs = back((3, 2), dq, extra=(got[7], got[6]))
    give_back((3, 2), outs)
    q_a, sum_1 = back((1,), dq, 0, split, True, None, True)
    handed_a = shifted(q_a, "section", -1)
    dq, out = back((1,), dq, split, split, False, sum_1, False, (got[5], got[4]))
    give_back((1,), [out])

    def final(*refs):
        final_kernel(split, split, *refs)

    q_b, own = call(
        final, "own_last", 0.4, (*common, ld, kv, dq, own), [half, PAIR],
        [pltpu.VMEM((split * HD, ROWS), F32)] + own_scratch, (got[3], got[2]),
    )
    handed_b = shifted(q_b, "section", -1)
    total = own
    for d in (7, 6, 5, 4, 3, 2, 1):
        total = total + got[d].astype(F32)
    kv_g = shifted(total.astype(BF16), "section", -1)
    return (jnp.concatenate([handed_a, handed_b], axis=1)[None], kv_g[None, :, :HD], kv_g[None, :, HD:])


def solution(mesh):
    wide = P("section", "ctx", None)
    in_specs = (wide, wide, wide, wide, wide, wide, P("section", "ctx"))
    return jax.shard_map(per_device, mesh=mesh, in_specs=in_specs, out_specs=(wide, wide, wide), check_vma=False)
```

```python
import math

import jax
import jax.numpy as jnp
from jax import lax
from jax.experimental import pallas as pl
from jax.experimental.pallas import tpu as pltpu
from jax.sharding import PartitionSpec as P

HEADS = 8
HD = 128
ROWS = 512
HALF = 256
SCALE = HD**-0.5
LOG2E = math.log2(math.e)
F32 = jnp.float32
BF16 = jnp.bfloat16
LSE, DELTA, LSE_BACK = 0, HEADS, 2 * HEADS
FAR = 4
SPLIT = 6
UNROLL = 4
WIDE = jax.ShapeDtypeStruct((HEADS * HD, ROWS), F32)
PAIR = jax.ShapeDtypeStruct((ROWS, 2 * HD), F32)


def dot(a, b, da, db):
    return lax.dot_general(a, b, (((da,), (db,)), ((), ())), preferred_element_type=F32)


def lanes(h):
    return pl.ds(pl.multiple_of(h * HD, HD), HD)


def terms(refs, h, to_h, lse_at, keys_at, n_keys, rows, ok):
    q_ref, do_ref, ld_ref, kv_ref, kt_ref, dq_ref, dk_ref, dv_ref = refs
    here = pl.ds(keys_at, n_keys)
    q = q_ref[rows, lanes(h)]
    do = do_ref[rows, lanes(h)]
    x = dot(kv_ref[here, :HD], q, 1, 1) * (SCALE * LOG2E) - ld_ref[pl.ds(lse_at + h, 1), rows]
    p = jnp.exp2(x)
    if ok is not None:
        p = jnp.where(ok, p, 0.0)
    dp = dot(kv_ref[here, HD:], do, 1, 1) - ld_ref[pl.ds(DELTA + h, 1), rows]
    ds = (p * dp).astype(BF16)
    dv_ref[here, :] += dot(p.astype(BF16), do, 1, 0)
    dk_ref[here, :] += dot(ds, q, 1, 0)
    dq_ref[lanes(to_h), rows] += dot(kt_ref[:, here], ds, 1, 0)


def finish(dq_ref, q_out):
    for h in range(q_out.shape[1] // HD):
        cols = slice(h * HD, (h + 1) * HD)
        q_out[:, cols] = (dq_ref[cols, :] * SCALE).astype(BF16).T


def own_terms(first, n, to, start_row, base, refs):
    kv_ref, kt_ref = refs[3], refs[4]
    kt_ref[...] = kv_ref[:, :HD].T

    def head(h, carry):
        for at, rows in ((0, slice(0, ROWS)), (HALF, slice(HALF, ROWS))):
            n_rows = rows.stop - rows.start
            key = lax.broadcasted_iota(jnp.int32, (HALF, n_rows), 0)
            ok = key >= start_row[:, rows] - (base + at)
            ok = ok & (key + (at - rows.start) <= lax.broadcasted_iota(jnp.int32, (HALF, n_rows), 1))
            terms(refs, h, h - to, LSE, at, HALF, rows, ok)
        return carry

    lax.fori_loop(first, first + n, head, 0)


def first_kernel(n, base_ref, starts, start_row, q_ref, do_ref, o_ref, lse_ref, kv_ref, ld_ref, dq_ref, out_ref, copy_ref, kt_ref, dk_ref, dv_ref):
    copy_ref[...] = kv_ref[...]
    lse = lse_ref[...] * LOG2E
    ld_ref[LSE : LSE + HEADS, :] = lse
    ld_ref[LSE_BACK : LSE_BACK + HEADS, :] = jnp.where(start_row[...] == starts[0, 0], lse, 1e30)
    ones = jnp.ones((8, HD), BF16)
    for h in range(HEADS):
        cols = slice(h * HD, (h + 1) * HD)
        x = do_ref[:, cols].astype(F32) * o_ref[:, cols].astype(F32)
        hi = x.astype(BF16)
        lo = (x - hi.astype(F32)).astype(BF16)
        row = dot(ones, hi, 1, 1) + dot(ones, lo, 1, 1)
        ld_ref[DELTA + h : DELTA + h + 1, :] = row[:1]
    dq_ref[...] = jnp.zeros_like(dq_ref)
    dk_ref[...] = jnp.zeros_like(dk_ref)
    dv_ref[...] = jnp.zeros_like(dv_ref)
    own_terms(0, n, 0, start_row, base_ref[0], (q_ref, do_ref, ld_ref, kv_ref, kt_ref, dq_ref, dk_ref, dv_ref))
    out_ref[:, :HD] = dk_ref[...]
    out_ref[:, HD:] = dv_ref[...]


def last_kernel(first, base_ref, starts, start_row, q_ref, do_ref, ld_ref, kv_ref, dq_in, sum_in, far_ref, part_ref, q_out, out_ref, passed_ref, dq_ref, kt_ref, dk_ref, dv_ref):
    dq_ref[...] = dq_in[first * HD :, :]
    dk_ref[...] = sum_in[:, :HD]
    dv_ref[...] = sum_in[:, HD:]
    own_terms(first, HEADS - first, first, start_row, base_ref[0], (q_ref, do_ref, ld_ref, kv_ref, kt_ref, dq_ref, dk_ref, dv_ref))
    finish(dq_ref, q_out)
    passed_ref[...] = far_ref[...].astype(F32) + part_ref[:ROWS, :].astype(F32)
    out_ref[:, :HD] = dk_ref[...] * SCALE + part_ref[ROWS:, :HD].astype(F32)
    out_ref[:, HD:] = dv_ref[...] + part_ref[ROWS:, HD:].astype(F32)


def back_kernel(ds, emit, joined, send, base_ref, starts, start_row, q_ref, do_ref, ld_ref, dq_in, *rest):
    m = len(ds)
    kv_in, rest = rest[:m], rest[m:]
    *rest, kv_ref, kt_ref, dk_ref, dv_ref = rest
    for i in range(send):
        rest[i - send][...] = rest[joined + i][...]
    rest = rest[: len(rest) - send]
    if emit:
        *rest, q_out = rest
    dq_ref, *out_refs = rest[-1 - m :] if emit else rest[-2:]
    base, start = base_ref[0], starts[0, 0]
    dk_ref[...] = jnp.zeros_like(dk_ref)
    dv_ref[...] = jnp.zeros_like(dv_ref)
    if joined:
        out_refs[0][m * ROWS :, :] = rest[0][...]
    reach = lax.shift_right_logical(base - start + (ROWS - 1), 9)
    skipped = sum((d > reach).astype(jnp.int32) for d in ds)
    refs = (q_ref, do_ref, ld_ref, kv_ref, kt_ref, dq_ref, dk_ref, dv_ref)

    def seen(d, width):
        key = lax.broadcasted_iota(jnp.int32, (ROWS, width), 0)
        return key >= start - (base - d * ROWS)

    @pl.when(skipped < m)
    def _():
        for b, d in enumerate(ds):
            here = slice(b * ROWS, (b + 1) * ROWS)
            kv = kv_in[b][...].astype(F32)
            kv_ref[here, :] = jnp.where(seen(d, 2 * HD), kv, kv[ROWS - 1 :, :]).astype(BF16)
            kt_ref[:, here] = jnp.where(seen(d, HD), kv[:, :HD], 0.0).astype(BF16).T

        def step(w, carry):
            w = w * UNROLL
            keys_at = pl.multiple_of((skipped + w // HEADS) * ROWS, ROWS)
            for i in range(UNROLL):
                h = w % HEADS + i
                terms(refs, h, h, LSE_BACK, keys_at, ROWS, slice(0, ROWS), None)
            return carry

        lax.fori_loop(0, (m - skipped) * (HEADS // UNROLL), step, 0)

    for b, d in enumerate(ds):
        here = slice(b * ROWS, (b + 1) * ROWS)
        ok = seen(d, HD)
        out_ref, to = (out_refs[b], slice(0, ROWS)) if emit else (out_refs[0], here)
        out_ref[to, :HD] = jnp.where(ok, dk_ref[here, :] * SCALE, 0.0).astype(BF16)
        out_ref[to, HD:] = jnp.where(ok, dv_ref[here, :], 0.0).astype(BF16)
    if emit:
        finish(dq_ref, q_out)


def work(pairs):
    flops = int(pairs * 5 * 2 * ROWS * ROWS * HD * HEADS * 0.05)
    return pl.CostEstimate(flops=flops, bytes_accessed=1 << 10, transcendentals=0)


def scratch(m):
    return [pltpu.VMEM((HD, m * ROWS), BF16), pltpu.VMEM((m * ROWS, HD), F32), pltpu.VMEM((m * ROWS, HD), F32)]


def call(kernel, name, pairs, scalars, operands, outs, scratch_shapes=(), aliases=None):
    return pl.pallas_call(
        kernel,
        out_shape=outs,
        in_specs=[pl.BlockSpec(memory_space=pltpu.SMEM)] * len(scalars) + [pl.BlockSpec(memory_space=pltpu.VMEM)] * len(operands),
        out_specs=[pl.BlockSpec(memory_space=pltpu.VMEM)] * len(outs),
        input_output_aliases=aliases or {},
        scratch_shapes=list(scratch_shapes),
        compiler_params=pltpu.CompilerParams(vmem_limit_bytes=24 << 20),
        cost_estimate=work(pairs),
        name=name,
    )(*scalars, *operands)


def shifted(block, axis, distance):
    devices = range(lax.axis_size(axis))
    route = [((i - distance) % len(devices), i) for i in devices]
    return lax.ppermute(block, axis, route)


def sum_kernel(total_ref, back_2, *rest):
    *arrays, out_ref = rest
    total = total_ref[...] + back_2[ROWS:, :].astype(F32)
    for array in arrays[:3]:
        total += array[...].astype(F32)
    out_ref[...] = total.astype(BF16)


def per_device(queries, keys, values, outputs, out_grads, lse, doc_start):
    q, do = queries[0], out_grads[0]
    base = (lax.axis_index("ctx") * ROWS).astype(jnp.int32)[None]
    kv = jnp.concatenate([keys[0], values[0]], axis=1)
    part = jax.ShapeDtypeStruct((ROWS, 2 * HD), BF16)
    pair = jax.ShapeDtypeStruct((2 * ROWS, 2 * HD), BF16)
    stats = jax.ShapeDtypeStruct((3 * HEADS, ROWS), F32)
    q_first = jax.ShapeDtypeStruct((ROWS, SPLIT * HD), BF16)
    q_last = jax.ShapeDtypeStruct((ROWS, (HEADS - SPLIT) * HD), BF16)
    scalars = (base, doc_start)

    def to_come(block, by):
        return shifted(block, "ctx", by)

    def first(*refs):
        first_kernel(SPLIT, *refs)

    held = {1: to_come(kv, 1), FAR: to_come(kv, FAR)}
    ld, dq, own, copy = call(
        first, "own_first", 0.6, scalars, (doc_start, q, do, outputs[0], lse[0].T, kv), [stats, WIDE, PAIR, part], scratch(1)
    )
    common = (doc_start, q, do, ld)

    def back(ds, dq, joined=(), emit=0, send=()):
        def kernel(*refs):
            back_kernel(ds, emit, len(joined), len(send), *refs)

        m = len(ds)
        outs = [part] * m if emit else [pair if m + len(joined) == 2 else part]
        return call(
            kernel,
            "back_" + "_".join(map(str, ds)),
            m,
            scalars,
            (*common, dq, *[held[d] for d in ds], *joined, *send),
            [WIDE] + outs + [q_first] * (emit > 0) + [part] * len(send),
            [pltpu.VMEM((m * ROWS, 2 * HD), BF16)] + scratch(m),
            {6: 0},
        )

    held[2] = to_come(copy, 2)
    dq, sum_1, copy, one = back((1,), dq, send=(kv, held[1]))
    held[3] = to_come(copy, 3)
    held[5] = to_come(one, FAR)
    dq, sum_4, two = back((4,), dq, send=(held[2],))
    held[6] = to_come(two, FAR)
    dq, sums, three = back((5,), dq, joined=(sum_1,), send=(held[3],))
    held[7] = to_come(three, FAR)
    back_1 = shifted(sums, "ctx", -1)
    dq, sums = back((6, 2), dq)
    back_2 = shifted(sums, "ctx", -2)
    dq, sum_7, sum_3, q_a = back((7, 3), dq, emit=SPLIT)
    back_7 = shifted(sum_7, "ctx", -7)
    back_3 = shifted(sum_3, "ctx", -3)
    handed_a = shifted(q_a, "section", -1)

    def final(*refs):
        last_kernel(SPLIT, *refs)

    q_b, total, passed = call(
        final,
        "own_last",
        0.4,
        scalars,
        (*common, kv, dq, own, sum_4, back_1),
        [q_last, PAIR, PAIR],
        [pltpu.VMEM(((HEADS - SPLIT) * HD, ROWS), F32)] + scratch(1),
    )
    handed_b = shifted(q_b, "section", -1)
    back_4 = shifted((passed + back_2[:ROWS].astype(F32)).astype(BF16), "ctx", -FAR)
    (kv_g,) = call(sum_kernel, "sums", 0.1, (), (total, back_2, back_7, back_3, back_4, handed_a), [part])
    kv_g = shifted(kv_g, "section", -1)
    return (jnp.concatenate([handed_a, handed_b], axis=1)[None], kv_g[None, :, :HD], kv_g[None, :, HD:])


def solution(mesh):
    wide = P("section", "ctx", None)
    in_specs = (wide, wide, wide, wide, wide, wide, P("section", "ctx"))
    return jax.shard_map(per_device, mesh=mesh, in_specs=in_specs, out_specs=(wide, wide, wide), check_vma=False)
```

```python
import math

import jax
import jax.numpy as jnp
from jax import lax
from jax.experimental import pallas as pl
from jax.experimental.pallas import tpu as pltpu
from jax.sharding import PartitionSpec as P

HEADS = 8
HD = 128
ROWS = 512
HALF = 256
SCALE = HD**-0.5
LOG2E = math.log2(math.e)
F32 = jnp.float32
BF16 = jnp.bfloat16
LSE, DELTA, LSE_BACK = 0, HEADS, 2 * HEADS
FAR = 4
SPLIT = 6
UNROLL = 4
WIDE = jax.ShapeDtypeStruct((HEADS * HD, ROWS), F32)
PAIR = jax.ShapeDtypeStruct((ROWS, 2 * HD), F32)


def dot(a, b, da, db):
    return lax.dot_general(a, b, (((da,), (db,)), ((), ())), preferred_element_type=F32)


def lanes(h):
    return pl.ds(pl.multiple_of(h * HD, HD), HD)


def terms(refs, h, to_h, lse_at, keys_at, n_keys, rows, ok):
    q_ref, do_ref, ld_ref, kv_ref, kt_ref, dq_ref, dk_ref, dv_ref = refs
    here = pl.ds(keys_at, n_keys)
    q = q_ref[rows, lanes(h)]
    do = do_ref[rows, lanes(h)]
    x = dot(kv_ref[here, :HD], q, 1, 1) * (SCALE * LOG2E) - ld_ref[pl.ds(lse_at + h, 1), rows]
    p = jnp.exp2(x)
    if ok is not None:
        p = jnp.where(ok, p, 0.0)
    dp = dot(kv_ref[here, HD:], do, 1, 1) - ld_ref[pl.ds(DELTA + h, 1), rows]
    ds = (p * dp).astype(BF16)
    dv_ref[here, :] += dot(p.astype(BF16), do, 1, 0)
    dk_ref[here, :] += dot(ds, q, 1, 0)
    dq_ref[lanes(to_h), rows] += dot(kt_ref[:, here], ds, 1, 0)


def finish(dq_ref, q_out):
    for h in range(q_out.shape[1] // HD):
        cols = slice(h * HD, (h + 1) * HD)
        q_out[:, cols] = (dq_ref[cols, :] * SCALE).astype(BF16).T


def own_terms(first, n, to, start_row, base, refs):
    kv_ref, kt_ref = refs[3], refs[4]
    kt_ref[...] = kv_ref[:, :HD].T

    def head(h, carry):
        for at, rows in ((0, slice(0, ROWS)), (HALF, slice(HALF, ROWS))):
            n_rows = rows.stop - rows.start
            key = lax.broadcasted_iota(jnp.int32, (HALF, n_rows), 0)
            ok = key >= start_row[:, rows] - (base + at)
            ok = ok & (key + (at - rows.start) <= lax.broadcasted_iota(jnp.int32, (HALF, n_rows), 1))
            terms(refs, h, h - to, LSE, at, HALF, rows, ok)
        return carry

    lax.fori_loop(first, first + n, head, 0)


def first_kernel(starts, start_row, do_ref, o_ref, lse_ref, kv_ref, ld_ref, dq_ref, copy_ref):
    copy_ref[...] = kv_ref[...]
    lse = lse_ref[...] * LOG2E
    ld_ref[LSE : LSE + HEADS, :] = lse
    ld_ref[LSE_BACK : LSE_BACK + HEADS, :] = jnp.where(start_row[...] == starts[0, 0], lse, 1e30)
    ones = jnp.ones((8, HD), BF16)
    for h in range(HEADS):
        cols = slice(h * HD, (h + 1) * HD)
        x = do_ref[:, cols].astype(F32) * o_ref[:, cols].astype(F32)
        hi = x.astype(BF16)
        lo = (x - hi.astype(F32)).astype(BF16)
        row = dot(ones, hi, 1, 1) + dot(ones, lo, 1, 1)
        ld_ref[DELTA + h : DELTA + h + 1, :] = row[:1]
    dq_ref[...] = jnp.zeros_like(dq_ref)


def own_kernel(n, base_ref, starts, start_row, q_ref, do_ref, ld_ref, kv_ref, dq_in, dq_ref, out_ref, kt_ref, dk_ref, dv_ref):
    dk_ref[...] = jnp.zeros_like(dk_ref)
    dv_ref[...] = jnp.zeros_like(dv_ref)
    own_terms(0, n, 0, start_row, base_ref[0], (q_ref, do_ref, ld_ref, kv_ref, kt_ref, dq_ref, dk_ref, dv_ref))
    out_ref[:, :HD] = dk_ref[...]
    out_ref[:, HD:] = dv_ref[...]


def last_kernel(first, base_ref, starts, start_row, q_ref, do_ref, ld_ref, kv_ref, dq_in, sum_in, far_ref, part_ref, q_out, out_ref, passed_ref, dq_ref, kt_ref, dk_ref, dv_ref):
    dq_ref[...] = dq_in[first * HD :, :]
    dk_ref[...] = sum_in[:, :HD]
    dv_ref[...] = sum_in[:, HD:]
    own_terms(first, HEADS - first, first, start_row, base_ref[0], (q_ref, do_ref, ld_ref, kv_ref, kt_ref, dq_ref, dk_ref, dv_ref))
    finish(dq_ref, q_out)
    passed_ref[...] = far_ref[...].astype(F32) + part_ref[:ROWS, :].astype(F32)
    out_ref[:, :HD] = dk_ref[...] * SCALE + part_ref[ROWS:, :HD].astype(F32)
    out_ref[:, HD:] = dv_ref[...] + part_ref[ROWS:, HD:].astype(F32)


def back_kernel(ds, emit, joined, send, base_ref, starts, start_row, q_ref, do_ref, ld_ref, dq_in, *rest):
    m = len(ds)
    kv_in, rest = rest[:m], rest[m:]
    *rest, kv_ref, kt_ref, dk_ref, dv_ref = rest
    for i in range(send):
        rest[i - send][...] = rest[joined + i][...]
    rest = rest[: len(rest) - send]
    if emit:
        *rest, q_out = rest
    dq_ref, *out_refs = rest[-1 - m :] if emit else rest[-2:]
    base, start = base_ref[0], starts[0, 0]
    dk_ref[...] = jnp.zeros_like(dk_ref)
    dv_ref[...] = jnp.zeros_like(dv_ref)
    if joined:
        out_refs[0][m * ROWS :, :] = rest[0][...]
    reach = lax.shift_right_logical(base - start + (ROWS - 1), 9)
    skipped = sum((d > reach).astype(jnp.int32) for d in ds)
    refs = (q_ref, do_ref, ld_ref, kv_ref, kt_ref, dq_ref, dk_ref, dv_ref)

    def seen(d, width):
        key = lax.broadcasted_iota(jnp.int32, (ROWS, width), 0)
        return key >= start - (base - d * ROWS)

    @pl.when(skipped < m)
    def _():
        for b, d in enumerate(ds):
            here = slice(b * ROWS, (b + 1) * ROWS)
            kv = kv_in[b][...].astype(F32)
            kv_ref[here, :] = jnp.where(seen(d, 2 * HD), kv, kv[ROWS - 1 :, :]).astype(BF16)
            kt_ref[:, here] = jnp.where(seen(d, HD), kv[:, :HD], 0.0).astype(BF16).T

        def step(w, carry):
            w = w * UNROLL
            keys_at = pl.multiple_of((skipped + w // HEADS) * ROWS, ROWS)
            for i in range(UNROLL):
                h = w % HEADS + i
                terms(refs, h, h, LSE_BACK, keys_at, ROWS, slice(0, ROWS), None)
            return carry

        lax.fori_loop(0, (m - skipped) * (HEADS // UNROLL), step, 0)

    for b, d in enumerate(ds):
        here = slice(b * ROWS, (b + 1) * ROWS)
        ok = seen(d, HD)
        out_ref, to = (out_refs[b], slice(0, ROWS)) if emit else (out_refs[0], here)
        out_ref[to, :HD] = jnp.where(ok, dk_ref[here, :] * SCALE, 0.0).astype(BF16)
        out_ref[to, HD:] = jnp.where(ok, dv_ref[here, :], 0.0).astype(BF16)
    if emit:
        finish(dq_ref, q_out)


def work(pairs):
    flops = int(pairs * 5 * 2 * ROWS * ROWS * HD * HEADS * 0.05)
    return pl.CostEstimate(flops=flops, bytes_accessed=1 << 10, transcendentals=0)


def scratch(m):
    return [pltpu.VMEM((HD, m * ROWS), BF16), pltpu.VMEM((m * ROWS, HD), F32), pltpu.VMEM((m * ROWS, HD), F32)]


def call(kernel, name, pairs, scalars, operands, outs, scratch_shapes=(), aliases=None):
    return pl.pallas_call(
        kernel,
        out_shape=outs,
        in_specs=[pl.BlockSpec(memory_space=pltpu.SMEM)] * len(scalars) + [pl.BlockSpec(memory_space=pltpu.VMEM)] * len(operands),
        out_specs=[pl.BlockSpec(memory_space=pltpu.VMEM)] * len(outs),
        input_output_aliases=aliases or {},
        scratch_shapes=list(scratch_shapes),
        compiler_params=pltpu.CompilerParams(vmem_limit_bytes=24 << 20),
        cost_estimate=work(pairs),
        name=name,
    )(*scalars, *operands)


def shifted(block, axis, distance):
    devices = range(lax.axis_size(axis))
    route = [((i - distance) % len(devices), i) for i in devices]
    return lax.ppermute(block, axis, route)


def sum_kernel(total_ref, back_2, *rest):
    *arrays, out_ref = rest
    total = total_ref[...] + back_2[ROWS:, :].astype(F32)
    for array in arrays[:3]:
        total += array[...].astype(F32)
    out_ref[...] = total.astype(BF16)


def per_device(queries, keys, values, outputs, out_grads, lse, doc_start):
    q, do = queries[0], out_grads[0]
    base = (lax.axis_index("ctx") * ROWS).astype(jnp.int32)[None]
    kv = jnp.concatenate([keys[0], values[0]], axis=1)
    part = jax.ShapeDtypeStruct((ROWS, 2 * HD), BF16)
    pair = jax.ShapeDtypeStruct((2 * ROWS, 2 * HD), BF16)
    stats = jax.ShapeDtypeStruct((3 * HEADS, ROWS), F32)
    q_first = jax.ShapeDtypeStruct((ROWS, SPLIT * HD), BF16)
    q_last = jax.ShapeDtypeStruct((ROWS, (HEADS - SPLIT) * HD), BF16)
    scalars = (base, doc_start)

    def to_come(block, by):
        return shifted(block, "ctx", by)

    def own_most(*refs):
        own_kernel(SPLIT, *refs)

    held = {1: to_come(kv, 1), FAR: to_come(kv, FAR)}
    ld, dq, copy = call(first_kernel, "statistics", 0.1, (doc_start,), (doc_start, do, outputs[0], lse[0].T, kv), [stats, WIDE, part])
    common = (doc_start, q, do, ld)

    def back(ds, dq, joined=(), emit=0, send=()):
        def kernel(*refs):
            back_kernel(ds, emit, len(joined), len(send), *refs)

        m = len(ds)
        outs = [part] * m if emit else [pair if m + len(joined) == 2 else part]
        return call(
            kernel,
            "back_" + "_".join(map(str, ds)),
            m,
            scalars,
            (*common, dq, *[held[d] for d in ds], *joined, *send),
            [WIDE] + outs + [q_first] * (emit > 0) + [part] * len(send),
            [pltpu.VMEM((m * ROWS, 2 * HD), BF16)] + scratch(m),
            {6: 0},
        )

    held[2] = to_come(copy, 2)
    dq, sum_1, copy, one = back((1,), dq, send=(kv, held[1]))
    held[3] = to_come(copy, 3)
    held[5] = to_come(one, FAR)
    dq, sum_4, two = back((4,), dq, send=(held[2],))
    held[6] = to_come(two, FAR)
    dq, own = call(own_most, "own_most", 0.6, scalars, (*common, kv, dq), [WIDE, PAIR], scratch(1), {7: 0})
    dq, sums, three = back((5,), dq, joined=(sum_1,), send=(held[3],))
    held[7] = to_come(three, FAR)
    back_1 = shifted(sums, "ctx", -1)
    dq, sums = back((6, 2), dq)
    back_2 = shifted(sums, "ctx", -2)
    dq, sum_7, sum_3, q_a = back((7, 3), dq, emit=SPLIT)
    back_7 = shifted(sum_7, "ctx", -7)
    back_3 = shifted(sum_3, "ctx", -3)
    handed_a = shifted(q_a, "section", -1)

    def final(*refs):
        last_kernel(SPLIT, *refs)

    q_b, total, passed = call(
        final,
        "own_last",
        0.4,
        scalars,
        (*common, kv, dq, own, sum_4, back_1),
        [q_last, PAIR, PAIR],
        [pltpu.VMEM(((HEADS - SPLIT) * HD, ROWS), F32)] + scratch(1),
    )
    handed_b = shifted(q_b, "section", -1)
    back_4 = shifted((passed + back_2[:ROWS].astype(F32)).astype(BF16), "ctx", -FAR)
    (kv_g,) = call(sum_kernel, "sums", 0.1, (), (total, back_2, back_7, back_3, back_4, handed_a), [part])
    kv_g = shifted(kv_g, "section", -1)
    return (jnp.concatenate([handed_a, handed_b], axis=1)[None], kv_g[None, :, :HD], kv_g[None, :, HD:])


def solution(mesh):
    wide = P("section", "ctx", None)
    in_specs = (wide, wide, wide, wide, wide, wide, P("section", "ctx"))
    return jax.shard_map(per_device, mesh=mesh, in_specs=in_specs, out_specs=(wide, wide, wide), check_vma=False)
```

```python
import math

import jax
import jax.numpy as jnp
from jax import lax
from jax.experimental import pallas as pl
from jax.experimental.pallas import tpu as pltpu
from jax.sharding import PartitionSpec as P

HEADS = 8
HD = 128
ROWS = 512
HALF = 256
SCALE = HD**-0.5
LOG2E = math.log2(math.e)
F32 = jnp.float32
BF16 = jnp.bfloat16
LSE, DELTA, LSE_BACK = 0, HEADS, 2 * HEADS
FAR = 4
SPLIT = 6
UNROLL = 4
WIDE = jax.ShapeDtypeStruct((HEADS * HD, ROWS), F32)
PAIR = jax.ShapeDtypeStruct((ROWS, 2 * HD), F32)


def dot(a, b, da, db):
    return lax.dot_general(a, b, (((da,), (db,)), ((), ())), preferred_element_type=F32)


def lanes(h):
    return pl.ds(pl.multiple_of(h * HD, HD), HD)


def terms(refs, h, to_h, lse_at, keys_at, n_keys, rows, ok):
    q_ref, do_ref, ld_ref, kv_ref, kt_ref, dq_ref, dk_ref, dv_ref = refs
    here = pl.ds(keys_at, n_keys)
    q = q_ref[rows, lanes(h)]
    do = do_ref[rows, lanes(h)]
    x = dot(kv_ref[here, :HD], q, 1, 1) * (SCALE * LOG2E) - ld_ref[pl.ds(lse_at + h, 1), rows]
    p = jnp.exp2(x)
    if ok is not None:
        p = jnp.where(ok, p, 0.0)
    dp = dot(kv_ref[here, HD:], do, 1, 1) - ld_ref[pl.ds(DELTA + h, 1), rows]
    ds = (p * dp).astype(BF16)
    dv_ref[here, :] += dot(p.astype(BF16), do, 1, 0)
    dk_ref[here, :] += dot(ds, q, 1, 0)
    dq_ref[lanes(to_h), rows] += dot(kt_ref[:, here], ds, 1, 0)


def finish(dq_ref, q_out):
    for h in range(q_out.shape[1] // HD):
        cols = slice(h * HD, (h + 1) * HD)
        q_out[:, cols] = (dq_ref[cols, :] * SCALE).astype(BF16).T


def own_terms(first, n, to, start_row, base, refs):
    kv_ref, kt_ref = refs[3], refs[4]
    kt_ref[...] = kv_ref[:, :HD].T

    def head(h, carry):
        for at, rows in ((0, slice(0, ROWS)), (HALF, slice(HALF, ROWS))):
            n_rows = rows.stop - rows.start
            key = lax.broadcasted_iota(jnp.int32, (HALF, n_rows), 0)
            ok = key >= start_row[:, rows] - (base + at)
            ok = ok & (key + (at - rows.start) <= lax.broadcasted_iota(jnp.int32, (HALF, n_rows), 1))
            terms(refs, h, h - to, LSE, at, HALF, rows, ok)
        return carry

    lax.fori_loop(first, first + n, head, 0)


def first_kernel(starts, start_row, do_ref, o_ref, lse_ref, kv_ref, ld_ref, dq_ref, copy_ref):
    copy_ref[...] = kv_ref[...]
    lse = lse_ref[...] * LOG2E
    ld_ref[LSE : LSE + HEADS, :] = lse
    ld_ref[LSE_BACK : LSE_BACK + HEADS, :] = jnp.where(start_row[...] == starts[0, 0], lse, 1e30)
    ones = jnp.ones((8, HD), BF16)
    for h in range(HEADS):
        cols = slice(h * HD, (h + 1) * HD)
        x = do_ref[:, cols].astype(F32) * o_ref[:, cols].astype(F32)
        hi = x.astype(BF16)
        lo = (x - hi.astype(F32)).astype(BF16)
        row = dot(ones, hi, 1, 1) + dot(ones, lo, 1, 1)
        ld_ref[DELTA + h : DELTA + h + 1, :] = row[:1]
    dq_ref[...] = jnp.zeros_like(dq_ref)


def own_kernel(n, base_ref, starts, start_row, q_ref, do_ref, ld_ref, kv_ref, dq_in, dq_ref, out_ref, kt_ref, dk_ref, dv_ref):
    dk_ref[...] = jnp.zeros_like(dk_ref)
    dv_ref[...] = jnp.zeros_like(dv_ref)
    own_terms(0, n, 0, start_row, base_ref[0], (q_ref, do_ref, ld_ref, kv_ref, kt_ref, dq_ref, dk_ref, dv_ref))
    out_ref[:, :HD] = dk_ref[...]
    out_ref[:, HD:] = dv_ref[...]


def last_kernel(first, base_ref, starts, start_row, q_ref, do_ref, ld_ref, kv_ref, dq_in, sum_in, far_ref, part_ref, q_out, out_ref, passed_ref, dq_ref, kt_ref, dk_ref, dv_ref):
    dq_ref[...] = dq_in[first * HD :, :]
    dk_ref[...] = sum_in[:, :HD]
    dv_ref[...] = sum_in[:, HD:]
    own_terms(first, HEADS - first, first, start_row, base_ref[0], (q_ref, do_ref, ld_ref, kv_ref, kt_ref, dq_ref, dk_ref, dv_ref))
    finish(dq_ref, q_out)
    passed_ref[...] = far_ref[...].astype(F32) + part_ref[:ROWS, :].astype(F32)
    out_ref[:, :HD] = dk_ref[...] * SCALE + part_ref[ROWS:, :HD].astype(F32)
    out_ref[:, HD:] = dv_ref[...] + part_ref[ROWS:, HD:].astype(F32)


def back_kernel(ds, emit, joined, send, base_ref, starts, start_row, q_ref, do_ref, ld_ref, dq_in, *rest):
    m = len(ds)
    kv_in, rest = rest[:m], rest[m:]
    *rest, kv_ref, kt_ref, dk_ref, dv_ref = rest
    for i in range(send):
        rest[i - send][...] = rest[joined + i][...]
    rest = rest[: len(rest) - send]
    if emit:
        *rest, q_out = rest
    dq_ref, *out_refs = rest[-1 - m :] if emit else rest[-2:]
    base, start = base_ref[0], starts[0, 0]
    dk_ref[...] = jnp.zeros_like(dk_ref)
    dv_ref[...] = jnp.zeros_like(dv_ref)
    if joined:
        out_refs[0][m * ROWS :, :] = rest[0][...]
    reach = lax.shift_right_logical(base - start + (ROWS - 1), 9)
    skipped = sum((d > reach).astype(jnp.int32) for d in ds)
    refs = (q_ref, do_ref, ld_ref, kv_ref, kt_ref, dq_ref, dk_ref, dv_ref)

    def seen(d, width):
        key = lax.broadcasted_iota(jnp.int32, (ROWS, width), 0)
        return key >= start - (base - d * ROWS)

    @pl.when(skipped < m)
    def _():
        for b, d in enumerate(ds):
            here = slice(b * ROWS, (b + 1) * ROWS)
            kv = kv_in[b][...].astype(F32)
            kv_ref[here, :] = jnp.where(seen(d, 2 * HD), kv, kv[ROWS - 1 :, :]).astype(BF16)
            kt_ref[:, here] = jnp.where(seen(d, HD), kv[:, :HD], 0.0).astype(BF16).T

        def step(w, carry):
            w = w * UNROLL
            keys_at = pl.multiple_of((skipped + w // HEADS) * ROWS, ROWS)
            for i in range(UNROLL):
                h = w % HEADS + i
                terms(refs, h, h, LSE_BACK, keys_at, ROWS, slice(0, ROWS), None)
            return carry

        lax.fori_loop(0, (m - skipped) * (HEADS // UNROLL), step, 0)

    for b, d in enumerate(ds):
        here = slice(b * ROWS, (b + 1) * ROWS)
        ok = seen(d, HD)
        out_ref, to = (out_refs[b], slice(0, ROWS)) if emit else (out_refs[0], here)
        out_ref[to, :HD] = jnp.where(ok, dk_ref[here, :] * SCALE, 0.0).astype(BF16)
        out_ref[to, HD:] = jnp.where(ok, dv_ref[here, :], 0.0).astype(BF16)
    if emit:
        finish(dq_ref, q_out)


def work(pairs):
    flops = int(pairs * 5 * 2 * ROWS * ROWS * HD * HEADS * 0.05)
    return pl.CostEstimate(flops=flops, bytes_accessed=1 << 10, transcendentals=0)


def scratch(m):
    return [pltpu.VMEM((HD, m * ROWS), BF16), pltpu.VMEM((m * ROWS, HD), F32), pltpu.VMEM((m * ROWS, HD), F32)]


def call(kernel, name, pairs, scalars, operands, outs, scratch_shapes=(), aliases=None):
    return pl.pallas_call(
        kernel,
        out_shape=outs,
        in_specs=[pl.BlockSpec(memory_space=pltpu.SMEM)] * len(scalars) + [pl.BlockSpec(memory_space=pltpu.VMEM)] * len(operands),
        out_specs=[pl.BlockSpec(memory_space=pltpu.VMEM)] * len(outs),
        input_output_aliases=aliases or {},
        scratch_shapes=list(scratch_shapes),
        compiler_params=pltpu.CompilerParams(vmem_limit_bytes=24 << 20),
        cost_estimate=work(pairs),
        name=name,
    )(*scalars, *operands)


def shifted(block, axis, distance):
    devices = range(lax.axis_size(axis))
    route = [((i - distance) % len(devices), i) for i in devices]
    return lax.ppermute(block, axis, route)


def sum_kernel(total_ref, back_2, *rest):
    *arrays, out_ref = rest
    total = total_ref[...] + back_2[ROWS:, :].astype(F32)
    for array in arrays[:3]:
        total += array[...].astype(F32)
    out_ref[...] = total.astype(BF16)


def per_device(queries, keys, values, outputs, out_grads, lse, doc_start):
    q, do = queries[0], out_grads[0]
    base = (lax.axis_index("ctx") * ROWS).astype(jnp.int32)[None]
    kv = jnp.concatenate([keys[0], values[0]], axis=1)
    part = jax.ShapeDtypeStruct((ROWS, 2 * HD), BF16)
    pair = jax.ShapeDtypeStruct((2 * ROWS, 2 * HD), BF16)
    stats = jax.ShapeDtypeStruct((3 * HEADS, ROWS), F32)
    q_first = jax.ShapeDtypeStruct((ROWS, SPLIT * HD), BF16)
    q_last = jax.ShapeDtypeStruct((ROWS, (HEADS - SPLIT) * HD), BF16)
    scalars = (base, doc_start)

    def to_come(block, by):
        return shifted(block, "ctx", by)

    def own_most(*refs):
        own_kernel(SPLIT, *refs)

    held = {1: to_come(kv, 1), FAR: to_come(kv, FAR)}
    ld, dq, copy = call(first_kernel, "statistics", 0.1, (doc_start,), (doc_start, do, outputs[0], lse[0].T, kv), [stats, WIDE, part])
    common = (doc_start, q, do, ld)

    def back(ds, dq, joined=(), emit=0, send=()):
        def kernel(*refs):
            back_kernel(ds, emit, len(joined), len(send), *refs)

        m = len(ds)
        outs = [part] * m if emit else [pair if m + len(joined) == 2 else part]
        return call(
            kernel,
            "back_" + "_".join(map(str, ds)),
            m,
            scalars,
            (*common, dq, *[held[d] for d in ds], *joined, *send),
            [WIDE] + outs + [q_first] * (emit > 0) + [part] * len(send),
            [pltpu.VMEM((m * ROWS, 2 * HD), BF16)] + scratch(m),
            {6: 0},
        )

    held[2] = to_come(copy, 2)
    dq, sum_1, copy, one = back((1,), dq, send=(kv, held[1]))
    held[3] = to_come(copy, 3)
    held[5] = to_come(one, FAR)
    dq, sum_4, two = back((4,), dq, send=(held[2],))
    held[6] = to_come(two, FAR)
    dq, own = call(own_most, "own_most", 0.6, scalars, (*common, kv, dq), [WIDE, PAIR], scratch(1), {7: 0})
    dq, sums, three = back((5,), dq, joined=(sum_1,), send=(held[3],))
    held[7] = to_come(three, FAR)
    back_1 = shifted(sums, "ctx", -1)
    dq, sums = back((6, 2), dq)
    back_2 = shifted(sums, "ctx", -2)
    dq, sum_7, sum_3, q_a = back((7, 3), dq, emit=SPLIT)
    handed_a = shifted(q_a, "section", -1)
    back_7 = shifted(sum_7, "ctx", -7)
    back_3 = shifted(sum_3, "ctx", -3)

    def final(*refs):
        last_kernel(SPLIT, *refs)

    q_b, total, passed = call(
        final,
        "own_last",
        0.4,
        scalars,
        (*common, kv, dq, own, sum_4, back_1),
        [q_last, PAIR, PAIR],
        [pltpu.VMEM(((HEADS - SPLIT) * HD, ROWS), F32)] + scratch(1),
    )
    handed_b = shifted(q_b, "section", -1)
    back_4 = shifted((passed + back_2[:ROWS].astype(F32)).astype(BF16), "ctx", -FAR)
    (kv_g,) = call(sum_kernel, "sums", 0.1, (), (total, back_2, back_7, back_3, back_4, handed_a), [part])
    kv_g = shifted(kv_g, "section", -1)
    return (jnp.concatenate([handed_a, handed_b], axis=1)[None], kv_g[None, :, :HD], kv_g[None, :, HD:])


def solution(mesh):
    wide = P("section", "ctx", None)
    in_specs = (wide, wide, wide, wide, wide, wide, P("section", "ctx"))
    return jax.shard_map(per_device, mesh=mesh, in_specs=in_specs, out_specs=(wide, wide, wide), check_vma=False)
```
